32 devices in a mesh: group: 8 (over z, y), tp: 4 (over x, core).
Axes of the slice: x: 2, y: 2, z: 4, core: 2. Of those that a mesh axis runs over, the one named last changes fastest.
Arguments:
- token_ids: int32 [2, 256], P(None, 'group'), may hold values from 0 to 1023
- row_counts: int32 [8], P('group'), may hold values from 8 to 32, as said below
- code_table: bfloat16 [1024, 5120], P(None, 'tp'), may hold values from -6 to 6
- x_weight: bfloat16 [5120, 10240], P('group', 'tp'), may hold values from -0.078125 to 0.078125
- z_weight: bfloat16 [5120, 10240], P('group', 'tp'), may hold values from -0.078125 to 0.078125
- dt_weight: bfloat16 [5120, 160], P('group', 'tp'), may hold values from -0.078125 to 0.078125
- bc_weight: bfloat16 [5120, 512], P('group', 'tp'), may hold values from -0.078125 to 0.078125
- dt_bias: float32 [160], P('tp'), may hold values from -3 to 0.5
- head_rate: float32 [160], P('tp'), may hold values from 0.05 to 8
- skip_gain: float32 [160], P('tp'), may hold values from 0.5 to 2
- norm_gain: float32 [10240], P('tp'), may hold values from 0.25 to 1.75
- out_weight: bfloat16 [10240, 5120], P('tp', 'group'), may hold values from -0.078125 to 0.078125
- ssm_state: bfloat16 [256, 160, 64, 256], P('group', 'tp')
Outputs:
- layer_out: bfloat16 [2, 256, 5120], P(None, 'group', 'tp')
The draws below stay inside these ranges and needn't reach their ends.
Inputs may be any that keep to these rules, and one draw needn't show every extreme that they name: `row_counts`: each count is a multiple of 8, and in every draw some group has all 32 rows live.
All inputs are finite; a program needn't handle non-finite values.
Results may differ from the reference program's by a relative error of at most 0.013.
Values may be sent and summed in bfloat16 or wider, within the bound.
A program may use at most 128 MiB of HBM per device.

```python
import math
import jax
import jax.numpy as jnp
from jax import lax

D = 5120
INNER = 10240
STATE = 256
HEADDIM = 64
CODES = 1024
ROWS = 32
HEADS = 160
GROUPS = 8


def draw_row_counts(key, part):
    first_key, second_key = jax.random.split(key, 2)
    values = 8 * jax.random.randint(first_key, (GROUPS,), 1, ROWS // 8 + 1)
    chosen = jax.random.randint(second_key, (), 0, GROUPS)
    return jnp.where(jnp.arange(GROUPS) == chosen, ROWS, values).astype(jnp.int32)


def draw_ssm_state(key, part):
    base_key, row_key = jax.random.split(key, 2)
    shape = (GROUPS * ROWS, HEADS, HEADDIM, STATE)
    position = jnp.arange(HEADS, dtype=jnp.float32) / max(HEADS - 1, 1)
    head_scale = jnp.exp(jnp.log(3.0) * position)
    row_scale = jnp.exp(jax.random.uniform(row_key, (GROUPS * ROWS,), minval=0.0, maxval=jnp.log(10.0)))
    base = jax.random.normal(base_key, shape)
    return (base * (row_scale[:, None, None, None] * head_scale[None, :, None, None] / 16.0)).astype(jnp.bfloat16)


def touch_ends(drawn, own_key, smallest, largest):
    longest = drawn.shape.index(max(drawn.shape))
    spots = []
    for shift in (0, 1):
        where = [jax.random.randint(jax.random.fold_in(own_key, axis), (), 0, length) for axis, length in enumerate(drawn.shape)]
        where[longest] = (where[longest] + shift) % drawn.shape[longest]
        spots.append(tuple(where))
    return drawn.at[spots[0]].set(smallest).at[spots[1]].set(largest)


def raised(values, key, source, target, shards_of, factor):
    def block_of(dim):
        return (jnp.arange(values.shape[dim]) // (values.shape[dim] // shards_of)).reshape((-1,) + (1,) * (values.ndim - 1 - dim))

    first = jax.random.permutation(key, shards_of)[block_of(target)]
    far = (block_of(target) + shards_of // 2) % shards_of
    return jnp.where((block_of(source) == first) | (block_of(source) == far), factor * values, values)


def block_scale(key, extent, shards, least, high):
    factor_of = 1.0
    for dim, parts in shards:
        draws = jax.random.uniform(jax.random.fold_in(jax.random.fold_in(key, 6), dim), (parts,), jnp.float32, least / len(shards), high / len(shards))
        factor_of = factor_of * jnp.repeat(jnp.exp(draws), extent[dim] // parts).reshape((-1,) + (1,) * (len(extent) - 1 - dim))
    return factor_of


def normal_values(stream_key, dims, spread, reach, shards=(), held_as=jnp.bfloat16):
    values = jax.random.normal(stream_key, dims, jnp.float32) * spread
    if len(shards) > 0:
        values = block_scale(stream_key, dims, shards, -0.22, 0.18) * values
    return jnp.clip(values, min=-reach, max=reach).astype(held_as)


def noise_with(key, shape, deviation, reach, cuts, heavy, kind=jnp.bfloat16):
    drawn = deviation * jax.random.normal(key, shape, jnp.float32)
    if cuts:
        drawn = drawn * block_scale(key, shape, cuts, -0.22, 0.18)
    return jnp.clip(raised(drawn, jax.random.fold_in(key, 3), *heavy), -reach, reach).astype(kind)


def setup_inputs(seed: int = 0) -> dict:
    keys = jax.random.split(jax.random.key(seed), 14)
    return {
        "token_ids": touch_ends(jax.random.randint(keys[0], (2, GROUPS * ROWS), 0, CODES), jax.random.fold_in(keys[0], 1), 0, CODES - 1).astype(jnp.int32),
        "row_counts": draw_row_counts(jax.random.fold_in(keys[13], 71), 0),
        "code_table": normal_values(keys[2], (CODES, D), 1.0, 6.0, ((1, 4),)),
        "x_weight": normal_values(keys[3], (D, INNER), D ** -0.5, 0.078125, ((0, 8), (1, 4))),
        "z_weight": normal_values(keys[4], (D, INNER), D ** -0.5, 0.078125, ((0, 8), (1, 4))),
        "dt_weight": normal_values(keys[5], (D, HEADS), D ** -0.5, 0.078125, ((0, 8), (1, 4))),
        "bc_weight": normal_values(keys[6], (D, 2 * STATE), D ** -0.5, 0.078125, ((0, 8), (1, 4))),
        "dt_bias": jnp.clip(-3.0 + 3.5 * jax.random.uniform(keys[7], (HEADS,), jnp.float32) ** block_scale(keys[7], (HEADS,), ((0, 4),), -0.2, 0.2), -3.0, 0.5),
        "head_rate": jnp.clip(jnp.exp(math.log(8.0) - 5.075174 * jax.random.uniform(keys[8], (HEADS,), jnp.float32) ** block_scale(keys[8], (HEADS,), ((0, 4),), -0.2, 0.2)), 0.05, 8.0),
        "skip_gain": jnp.clip(0.5 + 1.5 * jax.random.uniform(keys[9], (HEADS,), jnp.float32) ** block_scale(keys[9], (HEADS,), ((0, 4),), -0.2, 0.2), 0.5, 2.0),
        "norm_gain": jnp.clip(1.0 + 0.15 * jax.random.normal(keys[10], (INNER,), jnp.float32), 0.25, 1.75),
        "out_weight": noise_with(keys[11], (INNER, D), INNER ** -0.5, 0.078125, ((0, 4), (1, 8)), (0, 1, 8, 2.0)),
        "ssm_state": draw_ssm_state(jax.random.fold_in(keys[13], 71), 0),
    }


def decode(x_pre, z_pre, dt_pre, bc_all, dt_bias, head_rate, skip_gain, state):
    row_count = state.shape[0]
    head_count = state.shape[1]
    head_size = state.shape[2]
    width = bc_all.shape[1] // 2
    inputs = jax.nn.silu(x_pre).reshape(2, row_count, head_count, head_size)
    step_dt = jax.nn.softplus(dt_pre.reshape(2, row_count, head_count) + dt_bias)
    decay_factor = jnp.exp(-step_dt * head_rate)
    state_in = bc_all[:, :width].reshape(2, row_count, width)
    readout = bc_all[:, width:].reshape(2, row_count, width)
    carried = state.astype(jnp.float32)
    outputs = []
    for decode_step in range(2):
        carried = decay_factor[decode_step][:, :, None, None] * carried + (step_dt[decode_step][:, :, None] * inputs[decode_step])[..., None] * state_in[decode_step][:, None, None, :]
        reading = jnp.einsum('rhpn,rn->rhp', carried, readout[decode_step], precision=lax.Precision.HIGHEST)
        reading = reading + skip_gain[None, :, None] * inputs[decode_step]
        outputs.append(reading.reshape(row_count, head_count * head_size))
    return jnp.concatenate(outputs, 0) * jax.nn.silu(z_pre)

def reference(token_ids, row_counts, code_table, x_weight, z_weight, dt_weight, bc_weight, dt_bias, head_rate, skip_gain, norm_gain, out_weight, ssm_state):

    def one_group(group_index):
        begin = (group_index * ROWS).astype(jnp.int32)
        group_ids = lax.dynamic_slice_in_dim(token_ids, begin, ROWS, 1).reshape(-1)
        embed = jnp.take(code_table, group_ids, axis=0)
        x_pre = jnp.dot(embed, x_weight, preferred_element_type=jnp.float32)
        z_pre = jnp.dot(embed, z_weight, preferred_element_type=jnp.float32)
        dt_pre = jnp.dot(embed, dt_weight, preferred_element_type=jnp.float32)
        bc_all = jnp.dot(embed, bc_weight, preferred_element_type=jnp.float32)
        state = lax.dynamic_slice_in_dim(ssm_state, begin, ROWS, 0)
        gated = decode(x_pre, z_pre, dt_pre, bc_all, dt_bias, head_rate, skip_gain, state)
        squares = lax.optimization_barrier(jnp.sum(gated * gated, axis=1))
        scale = lax.rsqrt(squares / INNER + 1e-05)
        mixed = (gated * scale[:, None] * norm_gain).astype(jnp.bfloat16)
        result = embed.astype(jnp.float32) + jnp.dot(mixed, out_weight, preferred_element_type=jnp.float32)
        result = result.reshape(2, ROWS, D)
        live = jnp.arange(ROWS, dtype=jnp.int32) < row_counts[group_index]
        return jnp.where(live[None, :, None], result, 0.0).astype(jnp.bfloat16)
    stacked = lax.map(one_group, jnp.arange(GROUPS, dtype=jnp.int32))
    return jnp.transpose(stacked, (1, 0, 2, 3)).reshape(2, GROUPS * ROWS, D)
```

```python
import jax
import jax.numpy as jnp
from jax import lax
from jax.experimental import pallas as pl
from jax.experimental.pallas import tpu as pltpu
from jax.sharding import PartitionSpec as P

DOWN = 2.0**-32
UP = 2.0**32


def state_kernel(c_ref, s_ref, o_ref):
    for i in range(s_ref.shape[0]):
        prod = lax.dot_general(
            c_ref[i], s_ref[i], (((1,), (1,)), ((), ())), preferred_element_type=jnp.float32
        )
        o_ref[i] = prod[:8] + prod[8:]


def state_reads(readout, state):
    rows, chans, width = state.shape
    scaled = jnp.transpose(readout, (1, 0, 2)) * DOWN
    high = scaled.astype(jnp.bfloat16)
    low = (scaled - high.astype(jnp.float32)).astype(jnp.bfloat16)
    pad = ((0, 0), (0, 6), (0, 0))
    both = jnp.concatenate([jnp.pad(high, pad), jnp.pad(low, pad)], axis=1)
    step = 2
    return pl.pallas_call(
        state_kernel,
        grid=(rows // step,),
        in_specs=[
            pl.BlockSpec((step, 16, width), lambda i: (i, 0, 0)),
            pl.BlockSpec((step, chans, width), lambda i: (i, 0, 0)),
        ],
        out_specs=pl.BlockSpec((step, 8, chans), lambda i: (i, 0, 0)),
        out_shape=jax.ShapeDtypeStruct((rows, 8, chans), jnp.float32),
        compiler_params=pltpu.CompilerParams(vmem_limit_bytes=32 * 1024 * 1024),
        cost_estimate=pl.CostEstimate(
            flops=2 * 16 * rows * chans * width,
            bytes_accessed=2 * rows * chans * width,
            transcendentals=0,
        ),
    )(both, state)


def group_sum(partial, dtype):
    groups = lax.axis_size("group")
    moved = lax.all_to_all(partial.astype(dtype), "group", split_axis=0, concat_axis=0, tiled=True)
    return jnp.sum(moved.reshape(groups, -1, partial.shape[1]).astype(jnp.float32), axis=0)


def per_device(
    token_ids, row_counts, code_table, x_weight, z_weight, dt_weight, bc_weight,
    dt_bias, head_rate, skip_gain, norm_gain, out_weight, ssm_state,
):
    row_count = token_ids.shape[1]
    flat_ids = token_ids.reshape(-1)
    code_count = code_table.shape[0]
    tps = lax.axis_size("tp")
    one_hot = (flat_ids[:, None] == jnp.arange(code_count, dtype=jnp.int32)[None, :]).astype(
        jnp.bfloat16
    )
    own_embed = jnp.dot(one_hot, code_table, preferred_element_type=jnp.float32).astype(
        jnp.bfloat16
    )
    full_embed = lax.all_gather(own_embed, "tp", axis=1, tiled=True)
    sliced = lax.all_to_all(full_embed, "group", split_axis=1, concat_axis=0, tiled=True)
    heads = dt_weight.shape[1]
    chans = x_weight.shape[1]
    small = jnp.concatenate([dt_weight, bc_weight], axis=1)
    small_sum = group_sum(jnp.dot(sliced, small, preferred_element_type=jnp.float32), jnp.float32)
    dt_pre = small_sum[:, :heads]
    bc_all = lax.all_gather(small_sum[:, heads:], "tp", axis=1, tiled=True)
    width = bc_all.shape[1] // 2
    state_in = bc_all[:, :width].reshape(2, row_count, width)
    readout = bc_all[:, width:].reshape(2, row_count, width)
    x_pre = group_sum(jnp.dot(sliced, x_weight, preferred_element_type=jnp.float32), jnp.bfloat16)
    z_pre = group_sum(jnp.dot(sliced, z_weight, preferred_element_type=jnp.float32), jnp.bfloat16)
    held = state_reads(readout, ssm_state.reshape(row_count, chans, width))

    step_dt = jax.nn.softplus(dt_pre.reshape(2, row_count, heads) + dt_bias)
    decay = jnp.exp(-step_dt * head_rate)
    b0c0 = jnp.sum(state_in[0] * readout[0], axis=1)[:, None]
    b0c1 = jnp.sum(state_in[0] * readout[1], axis=1)[:, None]
    b1c1 = jnp.sum(state_in[1] * readout[1], axis=1)[:, None]
    spread = lambda a: jnp.repeat(a, chans // heads, axis=-1)
    inputs = jax.nn.silu(x_pre).reshape(2, row_count, chans)
    read0 = (held[:, 0] * spread(decay[0])) * UP + inputs[0] * spread(
        step_dt[0] * b0c0 + skip_gain
    )
    read1 = (
        (held[:, 1] * spread(decay[0] * decay[1])) * UP
        + inputs[0] * spread(decay[1] * step_dt[0] * b0c1)
        + inputs[1] * spread(step_dt[1] * b1c1 + skip_gain)
    )
    gated = jnp.concatenate([read0, read1], 0) * jax.nn.silu(z_pre)
    squares = lax.psum(jnp.sum(gated * gated, axis=1), "tp")
    scale = lax.rsqrt(squares / (chans * tps) + 1e-05)
    mixed = (gated * scale[:, None] * norm_gain).astype(jnp.bfloat16)
    all_mixed = lax.all_gather(mixed, "group", axis=0, tiled=True)
    partial_out = jnp.dot(all_mixed, out_weight, preferred_element_type=jnp.float32)
    mine = lax.all_to_all(
        partial_out.astype(jnp.bfloat16), "group", split_axis=0, concat_axis=1, tiled=True
    )
    parts = lax.all_to_all(mine, "tp", split_axis=1, concat_axis=0, tiled=True)
    summed = jnp.sum(parts.reshape(tps, 2 * row_count, -1).astype(jnp.float32), axis=0)
    result = (own_embed.astype(jnp.float32) + summed).reshape(2, row_count, summed.shape[1])
    live = jnp.arange(row_count, dtype=jnp.int32) < row_counts[0]
    return jnp.where(live[None, :, None], result, 0.0).astype(jnp.bfloat16)


def solution(mesh):
    return jax.shard_map(
        per_device,
        mesh=mesh,
        in_specs=(
            P(None, "group"), P("group"), P(None, "tp"),
            P("group", "tp"), P("group", "tp"), P("group", "tp"), P("group", "tp"),
            P("tp"), P("tp"), P("tp"), P("tp"),
            P("tp", "group"), P("group", "tp", None, None),
        ),
        out_specs=P(None, "group", "tp"),
        check_vma=False,
    )
```

```python
import jax
import jax.numpy as jnp
from jax import lax
from jax.experimental import pallas as pl
from jax.experimental.pallas import tpu as pltpu
from jax.sharding import PartitionSpec as P

DOWN = 2.0**-32
UP = 2.0**32


def state_kernel(c_ref, s_ref, o_ref):
    for i in range(s_ref.shape[0]):
        prod = lax.dot_general(
            c_ref[i], s_ref[i], (((1,), (1,)), ((), ())), preferred_element_type=jnp.float32
        )
        o_ref[i] = prod[:8] + prod[8:]


def state_reads(readout, state):
    rows, chans, width = state.shape
    scaled = jnp.transpose(readout, (1, 0, 2)) * DOWN
    high = scaled.astype(jnp.bfloat16)
    low = (scaled - high.astype(jnp.float32)).astype(jnp.bfloat16)
    pad = ((0, 0), (0, 6), (0, 0))
    both = jnp.concatenate([jnp.pad(high, pad), jnp.pad(low, pad)], axis=1)
    step = 2
    return pl.pallas_call(
        state_kernel,
        grid=(rows // step,),
        in_specs=[
            pl.BlockSpec((step, 16, width), lambda i: (i, 0, 0)),
            pl.BlockSpec((step, chans, width), lambda i: (i, 0, 0)),
        ],
        out_specs=pl.BlockSpec((step, 8, chans), lambda i: (i, 0, 0)),
        out_shape=jax.ShapeDtypeStruct((rows, 8, chans), jnp.float32),
        compiler_params=pltpu.CompilerParams(vmem_limit_bytes=32 * 1024 * 1024),
        cost_estimate=pl.CostEstimate(
            flops=2 * 16 * rows * chans * width,
            bytes_accessed=2 * rows * chans * width,
            transcendentals=0,
        ),
    )(both, state)


def group_sum(partial, dtype):
    groups = lax.axis_size("group")
    moved = lax.all_to_all(partial.astype(dtype), "group", split_axis=0, concat_axis=0, tiled=True)
    return jnp.sum(moved.reshape(groups, -1, partial.shape[1]).astype(jnp.float32), axis=0)


def pair_sum(keep, give, weight):
    groups = lax.axis_size("group")
    lines = groups // 2
    swap = [(i, i + 1 - 2 * (i % 2)) for i in range(groups)]
    given = jnp.dot(give, weight, preferred_element_type=jnp.float32).astype(jnp.bfloat16)
    got = lax.ppermute(given, "group", swap)
    kept = jnp.dot(keep, weight, preferred_element_type=jnp.float32)
    both = (kept + got.astype(jnp.float32)).astype(jnp.bfloat16)
    along = [[2 * i + j for i in range(lines)] for j in range(2)]
    moved = lax.all_to_all(
        both, "group", split_axis=0, concat_axis=0, axis_index_groups=along, tiled=True
    )
    return jnp.sum(moved.reshape(lines, -1, weight.shape[1]).astype(jnp.float32), axis=0)


def per_device(
    token_ids, row_counts, code_table, x_weight, z_weight, dt_weight, bc_weight,
    dt_bias, head_rate, skip_gain, norm_gain, out_weight, ssm_state,
):
    row_count = token_ids.shape[1]
    flat_ids = token_ids.reshape(-1)
    code_count = code_table.shape[0]
    tps = lax.axis_size("tp")
    one_hot = (flat_ids[:, None] == jnp.arange(code_count, dtype=jnp.int32)[None, :]).astype(
        jnp.bfloat16
    )
    own_embed = jnp.dot(one_hot, code_table, preferred_element_type=jnp.float32).astype(
        jnp.bfloat16
    )
    full_embed = lax.all_gather(own_embed, "tp", axis=1, tiled=True)
    sliced = lax.all_to_all(full_embed, "group", split_axis=1, concat_axis=0, tiled=True)
    side = lax.rem(lax.axis_index("group"), 2)
    pairs = sliced.reshape(-1, 2, 2 * row_count, sliced.shape[1])
    keep = jnp.where(side == 0, pairs[:, 0], pairs[:, 1]).reshape(-1, sliced.shape[1])
    give = jnp.where(side == 0, pairs[:, 1], pairs[:, 0]).reshape(-1, sliced.shape[1])
    heads = dt_weight.shape[1]
    chans = x_weight.shape[1]
    small = jnp.concatenate([dt_weight, bc_weight], axis=1)
    small_sum = group_sum(jnp.dot(sliced, small, preferred_element_type=jnp.float32), jnp.float32)
    dt_pre = small_sum[:, :heads]
    bc_all = lax.all_gather(small_sum[:, heads:], "tp", axis=1, tiled=True)
    width = bc_all.shape[1] // 2
    state_in = bc_all[:, :width].reshape(2, row_count, width)
    readout = bc_all[:, width:].reshape(2, row_count, width)
    x_pre = pair_sum(keep, give, x_weight)
    z_pre = pair_sum(keep, give, z_weight)
    held = state_reads(readout, ssm_state.reshape(row_count, chans, width))

    step_dt = jax.nn.softplus(dt_pre.reshape(2, row_count, heads) + dt_bias)
    decay = jnp.exp(-step_dt * head_rate)
    b0c0 = jnp.sum(state_in[0] * readout[0], axis=1)[:, None]
    b0c1 = jnp.sum(state_in[0] * readout[1], axis=1)[:, None]
    b1c1 = jnp.sum(state_in[1] * readout[1], axis=1)[:, None]
    spread = lambda a: jnp.repeat(a, chans // heads, axis=-1)
    inputs = jax.nn.silu(x_pre).reshape(2, row_count, chans)
    read0 = (held[:, 0] * spread(decay[0])) * UP + inputs[0] * spread(
        step_dt[0] * b0c0 + skip_gain
    )
    read1 = (
        (held[:, 1] * spread(decay[0] * decay[1])) * UP
        + inputs[0] * spread(decay[1] * step_dt[0] * b0c1)
        + inputs[1] * spread(step_dt[1] * b1c1 + skip_gain)
    )
    gated = jnp.concatenate([read0, read1], 0) * jax.nn.silu(z_pre)
    squares = lax.psum(jnp.sum(gated * gated, axis=1), "tp")
    scale = lax.rsqrt(squares / (chans * tps) + 1e-05)
    mixed = (gated * scale[:, None] * norm_gain).astype(jnp.bfloat16)
    all_mixed = lax.all_gather(mixed, "group", axis=0, tiled=True)
    partial_out = jnp.dot(all_mixed, out_weight, preferred_element_type=jnp.float32)
    mine = lax.all_to_all(
        partial_out.astype(jnp.bfloat16), "group", split_axis=0, concat_axis=0, tiled=True
    )
    parts = lax.all_to_all(mine, "tp", split_axis=0, concat_axis=0, tiled=True)
    summed = jnp.sum(
        parts.reshape(tps, -1, 2 * row_count, out_weight.shape[1]).astype(jnp.float32), axis=0
    )
    summed = jnp.transpose(summed, (1, 0, 2)).reshape(2 * row_count, -1)
    result = (own_embed.astype(jnp.float32) + summed).reshape(2, row_count, summed.shape[1])
    live = jnp.arange(row_count, dtype=jnp.int32) < row_counts[0]
    return jnp.where(live[None, :, None], result, 0.0).astype(jnp.bfloat16)


def solution(mesh):
    return jax.shard_map(
        per_device,
        mesh=mesh,
        in_specs=(
            P(None, "group"), P("group"), P(None, "tp"),
            P("group", "tp"), P("group", "tp"), P("group", "tp"), P("group", "tp"),
            P("tp"), P("tp"), P("tp"), P("tp"),
            P("tp", "group"), P("group", "tp", None, None),
        ),
        out_specs=P(None, "group", "tp"),
        check_vma=False,
    )
```
